256 devices in a mesh: blk: 128 (over z, x, y), auth: 2 (over core).
Axes of the slice: x: 4, y: 4, z: 8, core: 2. Of those that a mesh axis runs over, the one named last changes fastest.
Arguments:
- features: bfloat16 [16384, 1024], P('blk', 'auth'), may hold values from -6 to 6
- partners: int32 [128, 64], P('blk'), may hold values from 0 to 127, as said below
- tiles: bfloat16 [128, 64, 128, 128], P('blk'), may hold values from -0.046875 to 0.046875
- paper_w_in: bfloat16 [1024, 2048], P(None, 'auth'), may hold values from -0.1875 to 0.1875
- paper_w_out: bfloat16 [2048, 1024], P('auth'), may hold values from -0.125 to 0.125
- paper_gain: float32 [1024], replicated, may hold values from 0.5 to 1.5
- author_feats: bfloat16 [16384, 1024], P('blk', 'auth'), may hold values from -6 to 6
- assign: int32 [16384], P('blk'), may hold values from 0 to 127
- author_w_in: bfloat16 [1024, 2048], P(None, 'auth'), may hold values from -0.1875 to 0.1875
- author_w_out: bfloat16 [2048, 1024], P('auth'), may hold values from -0.125 to 0.125
- author_gain: float32 [1024], replicated, may hold values from 0.5 to 1.5
Outputs:
- paper_out: bfloat16 [16384, 1024], P('blk', 'auth')
- author_out: bfloat16 [16384, 1024], P('blk', 'auth')
The draws below stay inside these ranges and needn't reach their ends.
Inputs may be any that keep to these rules, and one draw needn't show every extreme that they name: `partners`: each row names 64 different blocks and never its own; block c names block b exactly when block b names block c.
All inputs are finite; a program needn't handle non-finite values.
Results may differ from the reference program's by a relative error of at most 0.013.
Values may be sent and summed in bfloat16 or wider, within the bound.
No kernel may reach another device: no remote copies, remote signals or barrier semaphores. Data moves between devices by JAX's collectives and lax.ppermute only.
A program may use at most 128 MiB of HBM per device.

```python
import jax
import jax.numpy as jnp
from jax import lax

D = 1024
FF = 2048
R = 128
A_DEV = 128
BLOCKS = 128
PAPERS = 16384
PARTNERS = 64
AUTHORS = 16384


def draw_partners(key, part):
    count = BLOCKS
    modulus = count - 1
    round_key = jax.random.fold_in(key, 11)
    label_key = jax.random.fold_in(key, 12)
    order_key = jax.random.fold_in(key, 13)
    chosen = jax.random.permutation(round_key, modulus)[:PARTNERS].astype(jnp.int32)
    labels = jax.random.permutation(label_key, count).astype(jnp.int32)
    vertex = jnp.arange(count, dtype=jnp.int32)[:, None]
    rounds = chosen[None, :]
    mirror = jnp.mod(2 * rounds - vertex, modulus)
    other = jnp.where(vertex == modulus, rounds, jnp.where(vertex == rounds, modulus, mirror))
    labelled = labels[other]
    inverse = jnp.argsort(labels)
    table = labelled[inverse]
    keys = jax.random.split(order_key, count)
    shuffles = jax.vmap(lambda single: jax.random.permutation(single, PARTNERS))(keys)
    return jnp.take_along_axis(table, shuffles, axis=1).astype(jnp.int32)


def with_ends(array, rng, low, top_value):
    index_at = [jax.random.randint(jax.random.fold_in(rng, axis), (), 0, length) for axis, length in enumerate(array.shape)]
    main_axis = array.shape.index(max(array.shape))
    next_to = index_at[:main_axis] + [(index_at[main_axis] + 1) % array.shape[main_axis]] + index_at[main_axis + 1:]
    return array.at[tuple(index_at)].set(low).at[tuple(next_to)].set(top_value)


def levels(stream_key, dims, cuts, low, largest):
    def one(axis_at, shards_of):
        steps = jax.random.uniform(jax.random.fold_in(jax.random.fold_in(stream_key, 6), axis_at), (shards_of,), jnp.float32, low / len(cuts), largest / len(cuts))
        return jnp.repeat(jnp.exp(steps), dims[axis_at] // shards_of).reshape((-1,) + (1,) * (len(dims) - axis_at - 1))

    factor_of = one(*cuts[0])
    for cut in cuts[1:]:
        factor_of = factor_of * one(*cut)
    return factor_of


def noise(key, extent, spread, most, shards=(), held_as=jnp.bfloat16):
    drawn = spread * jax.random.normal(key, extent, jnp.float32)
    if shards:
        drawn = drawn * levels(key, extent, shards, -0.22, 0.18)
    return jnp.clip(drawn, -most, most).astype(held_as)


def setup_inputs(seed: int = 0) -> dict:
    seeds = jax.random.split(jax.random.key(seed), 12)
    features = noise(seeds[0], (PAPERS, D), 1.0, 6.0, ((0, 128), (1, 2)))
    partners = draw_partners(jax.random.fold_in(seeds[11], 71), 0)
    tiles = noise(seeds[2], (BLOCKS, PARTNERS, R, R), (2 * PARTNERS * R) ** -0.5, 0.046875, ((0, 128),))
    paper_w_in = noise(seeds[3], (D, FF), D ** -0.5, 0.1875, ((1, 2),))
    paper_w_out = noise(seeds[4], (FF, D), FF ** -0.5, 0.125, ((0, 2),))
    paper_gain = jnp.clip(1.0 + 0.1 * jax.random.normal(seeds[5], (D,), jnp.float32), 0.5, 1.5)
    author_feats = noise(seeds[6], (AUTHORS, D), 1.0, 6.0, ((0, 128), (1, 2)))
    assign = with_ends(jax.random.randint(seeds[7], (PAPERS,), 0, A_DEV), jax.random.fold_in(seeds[7], 1), 0, A_DEV - 1).astype(jnp.int32)
    author_w_in = noise(seeds[8], (D, FF), D ** -0.5, 0.1875, ((1, 2),))
    author_w_out = noise(seeds[9], (FF, D), FF ** -0.5, 0.125, ((0, 2),))
    author_gain = jnp.clip(1.0 + 0.1 * jax.random.normal(seeds[10], (D,), jnp.float32), 0.5, 1.5)
    return {"features": features, "partners": partners, "tiles": tiles, "paper_w_in": paper_w_in, "paper_w_out": paper_w_out, "paper_gain": paper_gain, "author_feats": author_feats, "assign": assign, "author_w_in": author_w_in, "author_w_out": author_w_out, "author_gain": author_gain}


epsilon = 1e-06

def feed_forward(inputs, w_in, w_out, gain):
    values = inputs.astype(jnp.float32)
    square = lax.optimization_barrier(jnp.mean(values * values, axis=-1, keepdims=True))
    normed = (values * lax.rsqrt(square + epsilon) * gain).astype(jnp.bfloat16)
    hidden = jax.nn.silu(jnp.dot(normed, w_in, preferred_element_type=jnp.float32)).astype(jnp.bfloat16)
    return jnp.dot(hidden, w_out, preferred_element_type=jnp.float32)

def reference(features, partners, tiles, paper_w_in, paper_w_out, paper_gain, author_feats, assign, author_w_in, author_w_out, author_gain):
    blocks = features.reshape(BLOCKS, R, D)

    def block_sum(index):
        partner_ids = partners[index]
        linked = blocks[partner_ids].astype(jnp.float32)
        back_slot = jnp.argmax(partners[partner_ids] == index, axis=1).astype(jnp.int32)
        own_tiles = tiles[index].astype(jnp.float32)
        back_tiles = tiles[partner_ids, back_slot].astype(jnp.float32)
        forward = jnp.einsum('fij,fjd->fid', own_tiles, linked)
        reverse = jnp.einsum('fji,fjd->fid', back_tiles, linked)
        messages = (forward + reverse).astype(jnp.bfloat16)
        return lax.optimization_barrier(jnp.sum(messages.astype(jnp.float32), axis=0))
    gathered_sum = lax.map(block_sum, jnp.arange(BLOCKS, dtype=jnp.int32)).reshape(PAPERS, D)
    paper_pre = (features.astype(jnp.float32) + gathered_sum).astype(jnp.bfloat16)
    paper_mid = (paper_pre.astype(jnp.float32) + feed_forward(paper_pre, paper_w_in, paper_w_out, paper_gain)).astype(jnp.bfloat16)
    member = (assign.reshape(BLOCKS, 1, R) == jnp.arange(A_DEV, dtype=jnp.int32)[None, :, None]).astype(jnp.float32)
    author_sum = jnp.einsum('bar,brd->bad', member, paper_mid.reshape(BLOCKS, R, D).astype(jnp.float32))
    counts = lax.optimization_barrier(jnp.sum(member, axis=2))[:, :, None]
    average = (author_sum / jnp.maximum(counts, 1.0)).reshape(AUTHORS, D)
    author_pre = (author_feats.astype(jnp.float32) + average).astype(jnp.bfloat16)
    author_out = (author_pre.astype(jnp.float32) + feed_forward(author_pre, author_w_in, author_w_out, author_gain)).astype(jnp.bfloat16)
    returned = jnp.einsum('bar,bad->brd', member, author_out.reshape(BLOCKS, A_DEV, D).astype(jnp.float32)).reshape(PAPERS, D)
    paper_out = (paper_mid.astype(jnp.float32) + returned).astype(jnp.bfloat16)
    return (paper_out, author_out)
```

```python
import jax
import jax.numpy as jnp
from jax import lax
from jax.experimental import pallas as pl
from jax.experimental.pallas import tpu as pltpu
from jax.sharding import Mesh
from jax.sharding import PartitionSpec as P

epsilon = 1e-06
bf16 = jnp.bfloat16
f32 = jnp.float32
plane = ("x", "y")


def place_tiles(ids_ref, core_ref, tiles_ref, slots_ref):
    slots_ref[...] = jnp.zeros_like(slots_ref)
    plane_size = slots_ref.shape[0]
    rows = slots_ref.shape[1]
    per_core = slots_ref.shape[2] // rows

    def place(f, carry):
        partner = ids_ref[f]
        along = partner // plane_size
        spot = partner % plane_size
        mine = along // per_core == core_ref[0]
        for step in range(per_core):

            @pl.when(jnp.logical_and(mine, along % per_core == step))
            def _():
                slots_ref[spot, :, step * rows : (step + 1) * rows] = tiles_ref[f]

        return carry

    lax.fori_loop(0, tiles_ref.shape[0], place, 0)


def slots_of(partner_ids, core, tiles, plane_size, per_core):
    rows = tiles.shape[1]
    return pl.pallas_call(
        place_tiles,
        out_shape=jax.ShapeDtypeStruct((plane_size, rows, per_core * rows), bf16),
        in_specs=[
            pl.BlockSpec(memory_space=pltpu.SMEM),
            pl.BlockSpec(memory_space=pltpu.SMEM),
            pl.BlockSpec(memory_space=pltpu.VMEM),
        ],
        out_specs=pl.BlockSpec(memory_space=pltpu.VMEM),
        compiler_params=pltpu.CompilerParams(vmem_limit_bytes=24 * 2**20),
        name="place_tiles",
    )(partner_ids, core, tiles)


def swap(value):
    return lax.ppermute(value, "core", [(0, 1), (1, 0)])


def mlp(rows, w_in, w_in_far, w_out, w_out_far, gain):
    values = rows.astype(f32)
    square = jnp.mean(values * values, axis=-1, keepdims=True)
    normed = (values * lax.rsqrt(square + epsilon) * gain).astype(bf16)
    near = jax.nn.silu(jnp.dot(normed, w_in, preferred_element_type=f32)).astype(bf16)
    far = jax.nn.silu(jnp.dot(normed, w_in_far, preferred_element_type=f32)).astype(bf16)
    update = jnp.dot(near, w_out, preferred_element_type=f32) + jnp.dot(
        far, w_out_far, preferred_element_type=f32
    )
    return (values + update).astype(bf16)


def local(
    features,
    partners,
    tiles,
    paper_w_in,
    paper_w_out,
    paper_gain,
    author_feats,
    assign,
    author_w_in,
    author_w_out,
    author_gain,
):
    rows, half = features.shape
    depth = lax.axis_size("z")
    spots = lax.axis_size("x") * lax.axis_size("y")
    per_core = depth // 2
    core = lax.axis_index("core")
    first = core == 0

    h_plane = lax.all_gather(features, plane, axis=0, tiled=True)
    h_column = lax.all_gather(features, "z", axis=0, tiled=True)
    slots = slots_of(partners[0], core.astype(jnp.int32)[None], tiles[0], spots, per_core)
    weights = [swap(w) for w in (paper_w_in, paper_w_out, author_w_in, author_w_out)]
    author_far = swap(author_feats)
    mine = lax.all_to_all(slots, plane, 0, 0, tiled=True)
    mine = mine.reshape(spots * rows, per_core * rows)
    other = swap(mine)

    low = jnp.where(first, mine, other)
    high = jnp.where(first, other, mine)
    whole = jnp.concatenate([low, high], axis=1)
    out_plane = jnp.dot(whole, h_column, preferred_element_type=f32).astype(bf16)
    out_column = lax.dot_general(
        whole, h_plane, (((0,), (0,)), ((), ())), preferred_element_type=f32
    ).astype(bf16)
    from_column = lax.psum_scatter(out_column, "z", scatter_dimension=0, tiled=True)
    from_plane = lax.all_to_all(out_plane.reshape(spots, rows, half), plane, 0, 0, tiled=True)
    gathered = jnp.sum(from_plane.astype(f32), axis=0) + from_column.astype(f32)
    pre = (features.astype(f32) + gathered).astype(bf16)

    def joined(near, far):
        return jnp.concatenate(
            [jnp.where(first, near, far), jnp.where(first, far, near)], axis=1
        )

    paper_pre = joined(pre, swap(pre))
    paper_mid = mlp(paper_pre, paper_w_in, weights[0], paper_w_out, weights[1], paper_gain)
    member = assign[None, :] == jnp.arange(author_feats.shape[0], dtype=jnp.int32)[:, None]
    member_matrix = member.astype(bf16)
    author_sum = jnp.dot(member_matrix, paper_mid, preferred_element_type=f32)
    counts = jnp.sum(member.astype(f32), axis=1, keepdims=True)
    average = author_sum / jnp.maximum(counts, 1.0)
    author_pre = (joined(author_feats, author_far).astype(f32) + average).astype(bf16)
    author_all = mlp(author_pre, author_w_in, weights[2], author_w_out, weights[3], author_gain)
    author_out = jnp.where(first, author_all[:, :half], author_all[:, half:])
    own_mid = jnp.where(first, paper_mid[:, :half], paper_mid[:, half:])
    returned = jnp.dot(member_matrix.T, author_out, preferred_element_type=f32)
    paper_out = (own_mid.astype(f32) + returned).astype(bf16)
    return (paper_out, author_out)


def solution(mesh):
    chips = Mesh(mesh.devices.reshape(8, 4, 4, 2), ("z", "x", "y", "core"))
    blk = ("z", "x", "y")
    placed = (
        P(blk, "core"),
        P(blk, None),
        P(blk, None, None, None),
        P(None, "core"),
        P("core", None),
        P(),
        P(blk, "core"),
        P(blk),
        P(None, "core"),
        P("core", None),
        P(),
    )
    return jax.shard_map(
        local,
        mesh=chips,
        in_specs=placed,
        out_specs=(P(blk, "core"), P(blk, "core")),
        check_vma=False,
    )
```

```python
import functools
import itertools

import jax
import jax.numpy as jnp
from jax import lax
from jax.experimental import pallas as pl
from jax.experimental.pallas import tpu as pltpu
from jax.sharding import Mesh
from jax.sharding import PartitionSpec as P

epsilon = 1e-06
bf16 = jnp.bfloat16
f32 = jnp.float32
plane = ("x", "y")
SMEM = pl.BlockSpec(memory_space=pltpu.SMEM)
VMEM = pl.BlockSpec(memory_space=pltpu.VMEM)
HBM = pl.BlockSpec(memory_space=pltpu.HBM)
ANY = pl.BlockSpec(memory_space=pl.ANY)
MIB = 2**20


def lanes(start, size):
    return pl.ds(pl.multiple_of(start, 128), size)


def dot(left, right):
    return jnp.dot(left, right, preferred_element_type=f32)


def place_tiles(place, ids_ref, tiles_ref, *refs):
    slots_ref, held, arrived = refs[-3:]
    spots, rows, wide = slots_ref.shape
    per_core = wide // rows
    depth = 2 * per_core
    parts = 4
    size = tiles_ref.shape[0] // parts
    copies = [
        pltpu.make_async_copy(
            tiles_ref.at[pl.ds(i * size, size)], held.at[pl.ds(i * size, size)], arrived.at[i]
        )
        for i in range(parts)
    ]
    for copy in copies:
        copy.start()
    slots_ref[...] = jnp.zeros_like(slots_ref)

    def put(f, carry):
        partner = ids_ref[f]
        layer = partner // spots
        pair = (layer // 2 - place[1] // 2 + depth // 2) % (depth // 2)
        ahead = pair * 2 + layer % 2 - place[0] * per_core

        @pl.when(jnp.logical_and(ahead >= 0, ahead < per_core))
        def _():
            slots_ref[partner % spots, :, lanes(ahead * rows, rows)] = held[f]

        return carry

    for i, copy in enumerate(copies):
        copy.wait()
        lax.fori_loop(i * size, (i + 1) * size, put, 0)


def join_rows(*refs):
    blocks, out_ref = refs[:-1], refs[-1]
    rows = blocks[0].shape[1]
    for i, block in enumerate(blocks):
        for j in range(2):
            out_ref[(2 * i + j) * rows : (2 * i + j + 1) * rows, :] = block[j]


def chip_at(place, r, s, n=4):
    dx = jnp.where(place[0] == 0, r, s)
    dy = jnp.where(place[0] == 0, s, r)
    return (place[2] + n + dx) % n * n + (place[3] + n + dy) % n


def forward_sums(place, near_ref, far_ref, rhs_ref, *refs):
    outs, held, left = refs[:-2], refs[-2], refs[-1]
    width = near_ref.shape[1]
    n, rows, _ = outs[0].shape
    copies = []
    for r, out in enumerate(outs):
        at = [pl.ds(pl.multiple_of(chip_at(place, r, s) * rows, rows), rows) for s in range(n)]
        near = jnp.concatenate([near_ref[a, :] for a in at], axis=0)
        far = jnp.concatenate([far_ref[a, :] for a in at], axis=0)
        total = dot(near, rhs_ref[:width, :]) + dot(far, rhs_ref[width:, :])
        for s in range(n):
            held[r, s] = total[s * rows : (s + 1) * rows, :].astype(bf16)
        copies.append(pltpu.make_async_copy(held.at[r], out, left.at[r]))
        copies[-1].start()
    for copy in copies:
        copy.wait()


def add_first(*refs):
    came, kept, goes = refs[:4], refs[4], refs[5:]
    for s in range(4):
        total = came[0][s].astype(f32)
        for ref in came[1:]:
            total += ref[s].astype(f32)
        if s == 0:
            kept[...] = total
        else:
            goes[s - 1][...] = total.astype(bf16)


def plane_columns(place, *refs):
    pieces, out_ref = refs[:-1], refs[-1]
    n, _, rows = pieces[0].shape
    for r, piece in enumerate(pieces):
        for s in range(n):
            out_ref[:, lanes(chip_at(place, -r, -s) * rows, rows)] = piece[s]


def reverse_sums(place, lhs_ref, near_ref, far_ref, out_ref):
    depth, _, rows = out_ref.shape
    half = depth // 2
    for source, side in ((near_ref, place[0]), (far_ref, 1 - place[0])):
        for pair in range(half // 2):
            total = dot(lhs_ref[...], source[:, pair * 2 * rows : (pair + 1) * 2 * rows])
            for j in range(2):
                layer = (2 * (place[1] // 2) + pair * 2 + j + half * side) % depth
                out_ref[layer] = total[:, j * rows : (j + 1) * rows].astype(bf16)


def add_all(column_ref, features_ref, kept_ref, *refs):
    came, out_ref = refs[:-1], refs[-1]
    column = column_ref[0].astype(f32)
    for i in range(1, column_ref.shape[0]):
        column += column_ref[i].astype(f32)
    total = features_ref[...].astype(f32) + kept_ref[...] + column.T
    for ref in came:
        total += ref[...].astype(f32)
    out_ref[...] = total.astype(bf16)


def mlp(values, gain, held, copies, base):
    square = jnp.mean(values * values, axis=-1, keepdims=True)
    normed = (values * lax.rsqrt(square + epsilon) * gain[...]).astype(bf16)
    update = values
    for at in (base, base + 2):
        copies[at].wait()
        u = dot(normed, held[at])
        hidden = (u / (1.0 + jnp.exp(-u))).astype(bf16)
        copies[at + 1].wait()
        update += dot(hidden, held[at + 1])
    return update.astype(bf16)


def update_rows(
    place,
    pre_near,
    pre_far,
    author_near,
    author_far,
    assign_row,
    assign_column,
    paper_gain,
    author_gain,
    pw_in,
    pw_in_far,
    pw_out,
    pw_out_far,
    aw_in,
    aw_in_far,
    aw_out,
    aw_out_far,
    paper_out,
    author_out,
    joined,
    held,
    arrived,
):
    sources = (pw_in, pw_out, pw_in_far, pw_out_far, aw_in, aw_out, aw_in_far, aw_out_far)
    copies = [pltpu.make_async_copy(w, held.at[i], arrived.at[i]) for i, w in enumerate(sources)]
    for copy in copies:
        copy.start()
    half = pre_near.shape[1]
    near = lanes(place[0] * half, half)
    far = lanes((1 - place[0]) * half, half)
    joined[:, near] = pre_near[...].astype(f32)
    joined[:, far] = pre_far[...].astype(f32)
    mid = mlp(joined[...], paper_gain, held, copies, 0)
    count_rows = author_near.shape[0]
    papers = mid.shape[0]
    member = assign_row[...] == lax.broadcasted_iota(jnp.int32, (count_rows, papers), 0)
    counts = jnp.sum(member.astype(f32), axis=1, keepdims=True)
    average = dot(member.astype(bf16), mid) / jnp.maximum(counts, 1.0)
    joined[:, near] = author_near[...].astype(f32)
    joined[:, far] = author_far[...].astype(f32)
    author_pre = (joined[...] + average).astype(bf16).astype(f32)
    joined[...] = mid.astype(f32)
    own_mid = joined[:, near]
    final = mlp(author_pre, author_gain, held, copies, 4)
    joined[...] = final.astype(f32)
    own = joined[:, near].astype(bf16)
    author_out[...] = own
    of_paper = assign_column[...] == lax.broadcasted_iota(jnp.int32, (papers, count_rows), 1)
    paper_out[...] = (own_mid + dot(of_paper.astype(bf16), own)).astype(bf16)


def call(kernel, outs, smem, operands, left=(), after=(), scratch=(), limit=16, flops=0, name=None, out_specs=None):
    moved = sum(2 * a.size for a in (*operands, *left))

    def body(*refs):
        count = len(smem) + len(operands) + len(left)
        return kernel(*refs[:count], *refs[count + len(after) :])

    return pl.pallas_call(
        body,
        out_shape=outs,
        in_specs=[SMEM] * len(smem) + [VMEM] * len(operands) + [HBM] * len(left) + [ANY] * len(after),
        out_specs=out_specs or jax.tree.map(lambda _: VMEM, outs),
        scratch_shapes=list(scratch),
        compiler_params=pltpu.CompilerParams(vmem_limit_bytes=limit * MIB),
        cost_estimate=pl.CostEstimate(flops=flops, bytes_accessed=moved, transcendentals=0),
        name=name or kernel.__name__,
    )(*smem, *operands, *left, *after)


def sent(value, axes, target):
    sizes = [lax.axis_size(a) for a in axes]
    pairs = []
    for at in itertools.product(*(range(n) for n in sizes)):
        to = [i % n for i, n in zip(target(*at), sizes)]
        pairs.append((flat(at, sizes), flat(to, sizes)))
    return lax.ppermute(value, axes, pairs)


def flat(at, sizes):
    index = 0
    for i, n in zip(at, sizes):
        index = index * n + i
    return index


def swap(value):
    return sent(value, ("core",), lambda core: (core + 1,))


def along(value, by, first):
    def target(x, y, core):
        return (x, y + by, core) if (core == 0) == first else (x + by, y, core)

    return sent(value, ("x", "y", "core"), target)


def pair_ahead(pair, i, near):
    def target(z, core):
        return (z - 2 * (i + 2 * ((core == 0) != near)), core)

    return sent(pair, ("z", "core"), target)


def local(
    features,
    partners,
    tiles,
    paper_w_in,
    paper_w_out,
    paper_gain,
    author_feats,
    assign,
    author_w_in,
    author_w_out,
    author_gain,
):
    rows, half = features.shape
    depth = lax.axis_size("z")
    spots = lax.axis_size("x") * lax.axis_size("y")
    wide = depth // 2 * rows
    place = jnp.stack([lax.axis_index(a) for a in ("core", "z", "x", "y")]).astype(jnp.int32)

    turned = features.T
    lines = jnp.stack([turned] + [along(turned, s, True) for s in (1, 2, 3)])
    beside = sent(features, ("z",), lambda z: (z + 1 - 2 * (z % 2),))
    odd = lax.axis_index("z") % 2 == 1
    pair = jnp.stack([jnp.where(odd, beside, features), jnp.where(odd, features, beside)])
    slots = call(
        place_tiles,
        jax.ShapeDtypeStruct((spots, rows, wide), bf16),
        (place, partners[0]),
        (),
        (tiles[0],),
        (),
        [pltpu.VMEM(tiles[0].shape, bf16), pltpu.SemaphoreType.DMA((4,))],
        limit=8,
    )
    slots, pair, lines = lax.optimization_barrier((slots, pair, lines))
    by_plane = [lines] + [along(lines, r, False) for r in (1, 2, 3)]
    column = [pair_ahead(pair, i, near) for near in (True, False) for i in (0, 1)]
    near = lax.all_to_all(slots, plane, 0, 0, tiled=True).reshape(spots * rows, wide)
    linked = call(join_rows, jax.ShapeDtypeStruct((depth * rows, half), bf16), (), tuple(column))
    turned_plane = call(
        plane_columns,
        jax.ShapeDtypeStruct((half, spots * rows), bf16),
        (place,),
        tuple(by_plane),
    )
    near, linked, turned_plane = lax.optimization_barrier((near, linked, turned_plane))
    far = swap(near)
    cost = spots * rows * wide * half
    side = len(by_plane)
    line = jax.ShapeDtypeStruct((spots // side, rows, half), bf16)
    out_plane = call(
        forward_sums,
        [line] * side,
        (place,),
        (near, far, linked),
        (),
        (),
        [pltpu.VMEM((side, *line.shape), bf16), pltpu.SemaphoreType.DMA((side,))],
        limit=20,
        flops=4 * cost,
        out_specs=[HBM] * side,
    )
    to_lines = [out_plane[0]] + [along(out_plane[r], r, False) for r in range(1, side)]
    out_column = call(
        reverse_sums,
        jax.ShapeDtypeStruct((depth, half, rows), bf16),
        (place,),
        (turned_plane, near, far),
        (),
        (out_plane[0],),
        flops=4 * cost,
    )
    from_column = lax.all_to_all(out_column, "z", 0, 0, tiled=True)
    kept, *goes = call(
        add_first,
        [jax.ShapeDtypeStruct((rows, half), f32)]
        + [jax.ShapeDtypeStruct((rows, half), bf16)] * (side - 1),
        (),
        tuple(to_lines),
    )
    came = [along(v, s, True) for s, v in enumerate(goes, 1)]
    pre = call(
        add_all,
        jax.ShapeDtypeStruct((rows, half), bf16),
        (),
        (from_column, features, kept, *came),
    )
    weights = (paper_w_in, paper_w_out, author_w_in, author_w_out)
    both = [w for near_w in weights for w in (near_w, swap(near_w))]
    return call(
        update_rows,
        (jax.ShapeDtypeStruct((rows, half), bf16), jax.ShapeDtypeStruct((rows, half), bf16)),
        (place,),
        (
            pre,
            swap(pre),
            author_feats,
            swap(author_feats),
            assign[None, :],
            assign[:, None],
            paper_gain[None, :],
            author_gain[None, :],
        ),
        tuple(both),
        (),
        [
            pltpu.VMEM((rows, 2 * half), f32),
            pltpu.VMEM((8, 2 * half, 2 * half), bf16),
            pltpu.SemaphoreType.DMA((8,)),
        ],
        limit=58,
        flops=8 * rows * 4 * half * half * 4,
    )


def solution(mesh):
    chips = Mesh(mesh.devices.reshape(8, 4, 4, 2), ("z", "x", "y", "core"))
    blk = ("z", "x", "y")
    placed = (
        P(blk, "core"),
        P(blk, None),
        P(blk, None, None, None),
        P(None, "core"),
        P("core", None),
        P(),
        P(blk, "core"),
        P(blk),
        P(None, "core"),
        P("core", None),
        P(),
    )
    return jax.shard_map(
        local,
        mesh=chips,
        in_specs=placed,
        out_specs=(P(blk, "core"), P(blk, "core")),
        check_vma=False,
    )
```

```python
import functools
import itertools

import jax
import jax.numpy as jnp
from jax import lax
from jax.experimental import pallas as pl
from jax.experimental.pallas import tpu as pltpu
from jax.sharding import Mesh
from jax.sharding import PartitionSpec as P

epsilon = 1e-06
bf16 = jnp.bfloat16
f32 = jnp.float32
plane = ("x", "y")
SMEM = pl.BlockSpec(memory_space=pltpu.SMEM)
VMEM = pl.BlockSpec(memory_space=pltpu.VMEM)
HBM = pl.BlockSpec(memory_space=pltpu.HBM)
ANY = pl.BlockSpec(memory_space=pl.ANY)
MIB = 2**20


def lanes(start, size):
    return pl.ds(pl.multiple_of(start, 128), size)


def dot(left, right):
    return jnp.dot(left, right, preferred_element_type=f32)


def place_tiles(place, ids_ref, tiles_ref, *refs):
    slots_ref, held, arrived = refs[-3:]
    spots, rows, wide = slots_ref.shape
    per_core = wide // rows
    pairs = per_core
    parts = 4
    size = tiles_ref.shape[0] // parts
    copies = [
        pltpu.make_async_copy(
            tiles_ref.at[pl.ds(i * size, size)], held.at[pl.ds(i * size, size)], arrived.at[i]
        )
        for i in range(parts)
    ]
    for copy in copies:
        copy.start()
    slots_ref[...] = jnp.zeros_like(slots_ref)

    first_pair = pairs - (place[1] >> 1)
    first = place[0] * per_core

    def put(f, carry):
        partner = ids_ref[f]
        layer = partner >> spots.bit_length() - 1
        ahead = ((layer >> 1) + first_pair & pairs - 1) * 2 + (layer & 1) - first

        @pl.when((ahead >= 0) & (ahead < per_core))
        def _():
            slots_ref[partner & spots - 1, :, lanes(ahead * rows, rows)] = held[f]

        return carry

    for i, copy in enumerate(copies):
        copy.wait()
        lax.fori_loop(i * size, (i + 1) * size, put, 0, unroll=4)


def write_out(held, out_ref, written):
    copy = pltpu.make_async_copy(held, out_ref, written)
    copy.start()
    copy.wait()


def join_rows(place, *refs):
    blocks, out_ref, held, written = refs[:-3], *refs[-3:]
    rows = blocks[0].shape[1]
    count = len(blocks)
    for i, block in enumerate(blocks):
        spot = (i + place[0] * (count // 2)) % count * 2
        for j in range(2):
            held[pl.ds(pl.multiple_of((spot + j) * rows, rows), rows), :] = block[j]
    write_out(held, out_ref, written)


def chip_at(place, r, s, n=4):
    dx = jnp.where(place[0] == 0, r, s)
    dy = jnp.where(place[0] == 0, s, r)
    return (place[2] + n + dx) % n * n + (place[3] + n + dy) % n


def forward_sums(place, near_ref, far_ref, rhs_ref, *refs):
    outs, ready, held, left = refs[:-3], *refs[-3:]
    ready[...] = jnp.zeros_like(ready)
    width = near_ref.shape[1]
    n, rows, _ = outs[0].shape
    copies = []
    for r, out in enumerate(outs):
        at = [pl.ds(pl.multiple_of(chip_at(place, r, s) * rows, rows), rows) for s in range(n)]
        near = jnp.concatenate([near_ref[a, :] for a in at], axis=0)
        far = jnp.concatenate([far_ref[a, :] for a in at], axis=0)
        total = dot(near, rhs_ref[:width, :]) + dot(far, rhs_ref[width:, :])
        for s in range(n):
            held[r, s] = total[s * rows : (s + 1) * rows, :].astype(bf16)
        copies.append(pltpu.make_async_copy(held.at[r], out, left.at[r]))
        copies[-1].start()
    for copy in copies:
        copy.wait()


def add_first(*refs):
    came, kept, goes = refs[:4], refs[4], refs[5:]
    for s in range(4):
        total = came[0][s].astype(f32)
        for ref in came[1:]:
            total += ref[s].astype(f32)
        if s == 0:
            kept[...] = total
        else:
            goes[s - 1][...] = total.astype(bf16)


def reverse_sums(place, near_ref, far_ref, *refs):
    pieces, (out_ref, lhs_ref, held, written) = refs[:-4], refs[-4:]
    n, _, rows = pieces[0].shape
    for r, piece in enumerate(pieces):
        for s in range(n):
            lhs_ref[:, lanes(chip_at(place, -r, -s) * rows, rows)] = piece[s]
    depth = out_ref.shape[0]
    half = depth // 2
    copies = []
    for source, side in ((near_ref, place[0]), (far_ref, 1 - place[0])):
        for pair in range(half // 2):
            at = len(copies)
            total = dot(lhs_ref[...], source[:, pair * 2 * rows : (pair + 1) * 2 * rows])
            for j in range(2):
                held[2 * at + j] = total[:, j * rows : (j + 1) * rows].astype(bf16)
            layer = (2 * (place[1] // 2) + pair * 2 + half * side) % depth
            copies.append(
                pltpu.make_async_copy(
                    held.at[pl.ds(2 * at, 2)], out_ref.at[pl.ds(layer, 2)], written.at[at]
                )
            )
            copies[-1].start()
    for copy in copies:
        copy.wait()


def add_all(column_ref, features_ref, kept_ref, *refs):
    came, out_ref = refs[:-1], refs[-1]
    column = column_ref[0].astype(f32)
    for i in range(1, column_ref.shape[0]):
        column += column_ref[i].astype(f32)
    total = features_ref[...].astype(f32) + kept_ref[...] + column.T
    for ref in came:
        total += ref[...].astype(f32)
    out_ref[...] = total.astype(bf16)


def mlp(values, gain, held, copies, base):
    square = jnp.mean(values * values, axis=-1, keepdims=True)
    normed = (values * lax.rsqrt(square + epsilon) * gain[...]).astype(bf16)
    update = values
    for at in (base, base + 2):
        copies[at].wait()
        u = dot(normed, held[at])
        hidden = (u / (1.0 + jnp.exp(-u))).astype(bf16)
        copies[at + 1].wait()
        update += dot(hidden, held[at + 1])
    return update.astype(bf16)


def update_rows(
    place,
    pre_near,
    pre_far,
    author_near,
    author_far,
    assign_row,
    paper_gain,
    author_gain,
    pw_in,
    pw_in_far,
    pw_out,
    pw_out_far,
    aw_in,
    aw_in_far,
    aw_out,
    aw_out_far,
    paper_out,
    author_out,
    joined,
    held,
    arrived,
):
    sources = (pw_in, pw_out, pw_in_far, pw_out_far, aw_in, aw_out, aw_in_far, aw_out_far)
    copies = [pltpu.make_async_copy(w, held.at[i], arrived.at[i]) for i, w in enumerate(sources)]
    for copy in copies:
        copy.start()
    half = pre_near.shape[1]
    near = lanes(place[0] * half, half)
    far = lanes((1 - place[0]) * half, half)
    joined[:, near] = pre_near[...].astype(f32)
    joined[:, far] = pre_far[...].astype(f32)
    mid = mlp(joined[...], paper_gain, held, copies, 0)
    count_rows = author_near.shape[0]
    papers = mid.shape[0]
    member = assign_row[...] == lax.broadcasted_iota(jnp.int32, (count_rows, papers), 0)
    counts = jnp.sum(member.astype(f32), axis=1, keepdims=True)
    average = dot(member.astype(bf16), mid) / jnp.maximum(counts, 1.0)
    joined[:, near] = author_near[...].astype(f32)
    joined[:, far] = author_far[...].astype(f32)
    author_pre = (joined[...] + average).astype(bf16).astype(f32)
    joined[...] = mid.astype(f32)
    own_mid = joined[:, near]
    final = mlp(author_pre, author_gain, held, copies, 4)
    joined[...] = final.astype(f32)
    own = joined[:, near].astype(bf16)
    author_out[...] = own
    returned = lax.dot_general(
        member.astype(bf16), own, (((0,), (0,)), ((), ())), preferred_element_type=f32
    )
    paper_out[...] = (own_mid + returned).astype(bf16)


def call(kernel, outs, smem, operands, left=(), after=(), scratch=(), limit=16, flops=0, name=None, out_specs=None, moved=None):
    if moved is None:
        moved = sum(2 * a.size for a in (*operands, *left))

    def body(*refs):
        count = len(smem) + len(operands) + len(left)
        return kernel(*refs[:count], *refs[count + len(after) :])

    return pl.pallas_call(
        body,
        out_shape=outs,
        in_specs=[SMEM] * len(smem) + [VMEM] * len(operands) + [HBM] * len(left) + [ANY] * len(after),
        out_specs=out_specs or jax.tree.map(lambda _: VMEM, outs),
        scratch_shapes=list(scratch),
        compiler_params=pltpu.CompilerParams(vmem_limit_bytes=limit * MIB),
        cost_estimate=pl.CostEstimate(flops=flops, bytes_accessed=moved, transcendentals=0),
        name=name or kernel.__name__,
    )(*smem, *operands, *left, *after)


def sent(value, axes, target):
    sizes = [lax.axis_size(a) for a in axes]
    pairs = []
    for at in itertools.product(*(range(n) for n in sizes)):
        to = [i % n for i, n in zip(target(*at), sizes)]
        pairs.append((flat(at, sizes), flat(to, sizes)))
    return lax.ppermute(value, axes, pairs)


def flat(at, sizes):
    index = 0
    for i, n in zip(at, sizes):
        index = index * n + i
    return index


def swap(value):
    return sent(value, ("core",), lambda core: (core + 1,))


def along(value, by, first):
    def target(x, y, core):
        return (x, y + by, core) if (core == 0) == first else (x + by, y, core)

    return sent(value, ("x", "y", "core"), target)


def pair_ahead(pair, ahead):
    return sent(pair, ("z",), lambda z: (z - 2 * ahead,))


def local(
    features,
    partners,
    tiles,
    paper_w_in,
    paper_w_out,
    paper_gain,
    author_feats,
    assign,
    author_w_in,
    author_w_out,
    author_gain,
):
    rows, half = features.shape
    depth = lax.axis_size("z")
    spots = lax.axis_size("x") * lax.axis_size("y")
    wide = depth // 2 * rows
    place = jnp.stack([lax.axis_index(a) for a in ("core", "z", "x", "y")]).astype(jnp.int32)

    turned = features.T
    lines = jnp.stack([turned] + [along(turned, s, True) for s in (1, 2, 3)])
    beside = sent(features, ("z",), lambda z: (z + 1 - 2 * (z % 2),))
    odd = lax.axis_index("z") % 2 == 1
    pair = jnp.stack([jnp.where(odd, beside, features), jnp.where(odd, features, beside)])
    slots = call(
        place_tiles,
        jax.ShapeDtypeStruct((spots, rows, wide), bf16),
        (place, partners[0]),
        (),
        (tiles[0],),
        (),
        [pltpu.VMEM(tiles[0].shape, bf16), pltpu.SemaphoreType.DMA((4,))],
        limit=56,
    )
    author_far = swap(author_feats)
    slots, pair, lines, author_far = lax.optimization_barrier((slots, pair, lines, author_far))
    by_plane = [lines] + [along(lines, r, False) for r in (1, 2, 3)]
    column = [pair] + [pair_ahead(pair, i) for i in range(1, depth // 2)]
    near = lax.all_to_all(slots, plane, 0, 0, tiled=True).reshape(spots * rows, wide)
    linked = call(
        join_rows,
        pltpu.HBM((depth * rows, half), bf16),
        (place,),
        tuple(column),
        (),
        (by_plane[1], by_plane[3]),
        [pltpu.VMEM((depth * rows, half), bf16), pltpu.SemaphoreType.DMA],
        out_specs=HBM,
    )
    near, linked = lax.optimization_barrier((near, linked))
    far = swap(near)
    weights = (paper_w_in, paper_w_out, author_w_in, author_w_out)
    weights_far = [swap(w) for w in weights]
    cost = spots * rows * wide * half
    side = len(by_plane)
    line = pltpu.HBM((spots // side, rows, half), bf16)
    token = jax.ShapeDtypeStruct((8, 128), f32)
    *out_plane, ready = call(
        forward_sums,
        [line] * side + [token],
        (place,),
        (near, far, linked),
        (),
        (),
        [pltpu.VMEM((side, *line.shape), bf16), pltpu.SemaphoreType.DMA((side,))],
        limit=20,
        moved=0,
        out_specs=[HBM] * side + [VMEM],
    )
    to_lines = [out_plane[0]] + [along(out_plane[r], r, False) for r in range(1, side)]
    out_column = call(
        reverse_sums,
        pltpu.HBM((depth, half, rows), bf16),
        (place,),
        (near, far, *by_plane),
        (),
        (ready,),
        [
            pltpu.VMEM((half, spots * rows), bf16),
            pltpu.VMEM((depth, half, rows), bf16),
            pltpu.SemaphoreType.DMA((depth // 2,)),
        ],
        limit=20,
        flops=4 * cost,
        out_specs=HBM,
    )
    from_column = lax.all_to_all(out_column, "z", 0, 0, tiled=True)
    kept, *goes = call(
        add_first,
        [jax.ShapeDtypeStruct((rows, half), f32)]
        + [jax.ShapeDtypeStruct((rows, half), bf16)] * (side - 1),
        (),
        tuple(to_lines),
        (),
        tuple(weights_far[:2]),
    )
    came = [along(v, s, True) for s, v in enumerate(goes, 1)]
    pre = call(
        add_all,
        jax.ShapeDtypeStruct((rows, half), bf16),
        (),
        (from_column, features, kept, *came),
    )
    both = [w for pair_of in zip(weights, weights_far) for w in pair_of]
    return call(
        update_rows,
        (jax.ShapeDtypeStruct((rows, half), bf16), jax.ShapeDtypeStruct((rows, half), bf16)),
        (place,),
        (
            pre,
            swap(pre),
            author_feats,
            author_far,
            assign[None, :],
            paper_gain[None, :],
            author_gain[None, :],
        ),
        tuple(both),
        (),
        [
            pltpu.VMEM((rows, 2 * half), f32),
            pltpu.VMEM((8, 2 * half, 2 * half), bf16),
            pltpu.SemaphoreType.DMA((8,)),
        ],
        limit=58,
        flops=8 * rows * 4 * half * half * 4,
    )


def solution(mesh):
    chips = Mesh(mesh.devices.reshape(8, 4, 4, 2), ("z", "x", "y", "core"))
    blk = ("z", "x", "y")
    placed = (
        P(blk, "core"),
        P(blk, None),
        P(blk, None, None, None),
        P(None, "core"),
        P("core", None),
        P(),
        P(blk, "core"),
        P(blk),
        P(None, "core"),
        P("core", None),
        P(),
    )
    return jax.shard_map(
        local,
        mesh=chips,
        in_specs=placed,
        out_specs=(P(blk, "core"), P(blk, "core")),
        check_vma=False,
    )
```

```python
import functools
import itertools

import jax
import jax.numpy as jnp
from jax import lax
from jax.experimental import pallas as pl
from jax.experimental.pallas import tpu as pltpu
from jax.sharding import Mesh
from jax.sharding import PartitionSpec as P

epsilon = 1e-06
bf16 = jnp.bfloat16
f32 = jnp.float32
plane = ("x", "y")
SMEM = pl.BlockSpec(memory_space=pltpu.SMEM)
VMEM = pl.BlockSpec(memory_space=pltpu.VMEM)
HBM = pl.BlockSpec(memory_space=pltpu.HBM)
ANY = pl.BlockSpec(memory_space=pl.ANY)
MIB = 2**20


def lanes(start, size):
    return pl.ds(pl.multiple_of(start, 128), size)


def dot(left, right):
    return jnp.dot(left, right, preferred_element_type=f32)


def place_tiles(place, ids_ref, tiles_ref, *refs):
    slots_ref, held, arrived = refs[-3:]
    spots, rows, wide = slots_ref.shape
    per_core = wide // rows
    pairs = per_core
    parts = 4
    size = tiles_ref.shape[0] // parts
    copies = [
        pltpu.make_async_copy(
            tiles_ref.at[pl.ds(i * size, size)], held.at[pl.ds(i * size, size)], arrived.at[i]
        )
        for i in range(parts)
    ]
    for copy in copies:
        copy.start()
    slots_ref[...] = jnp.zeros_like(slots_ref)

    first_pair = pairs - (place[1] >> 1)
    first = place[0] * per_core

    def put(f, carry):
        partner = ids_ref[f]
        layer = partner >> spots.bit_length() - 1
        ahead = ((layer >> 1) + first_pair & pairs - 1) * 2 + (layer & 1) - first

        @pl.when((ahead >= 0) & (ahead < per_core))
        def _():
            slots_ref[partner & spots - 1, :, lanes(ahead * rows, rows)] = held[f]

        return carry

    for i, copy in enumerate(copies):
        copy.wait()
        lax.fori_loop(i * size, (i + 1) * size, put, 0, unroll=4)


def write_out(held, out_ref, written):
    copy = pltpu.make_async_copy(held, out_ref, written)
    copy.start()
    copy.wait()


def join_rows(place, *refs):
    blocks, out_ref, held, written = refs[:-3], *refs[-3:]
    rows = blocks[0].shape[1]
    count = len(blocks)
    for i, block in enumerate(blocks):
        spot = (i + place[0] * (count // 2)) % count * 2
        for j in range(2):
            held[pl.ds(pl.multiple_of((spot + j) * rows, rows), rows), :] = block[j]
    write_out(held, out_ref, written)


def chip_at(place, r, s, n=4):
    dx = jnp.where(place[0] == 0, r, s)
    dy = jnp.where(place[0] == 0, s, r)
    return (place[2] + n + dx) % n * n + (place[3] + n + dy) % n


def forward_sums(place, near_ref, far_ref, rhs_ref, *refs):
    outs, ready, held, left = refs[:-3], *refs[-3:]
    ready[...] = jnp.zeros_like(ready)
    width = near_ref.shape[1]
    n, rows, _ = outs[0].shape
    copies = []
    for r, out in enumerate(outs):
        at = [pl.ds(pl.multiple_of(chip_at(place, r, s) * rows, rows), rows) for s in range(n)]
        near = jnp.concatenate([near_ref[a, :] for a in at], axis=0)
        far = jnp.concatenate([far_ref[a, :] for a in at], axis=0)
        total = dot(near, rhs_ref[:width, :]) + dot(far, rhs_ref[width:, :])
        for s in range(n):
            held[r, s] = total[s * rows : (s + 1) * rows, :].astype(bf16)
        copies.append(pltpu.make_async_copy(held.at[r], out, left.at[r]))
        copies[-1].start()
    for copy in copies:
        copy.wait()


def add_first(*refs):
    came, kept, goes = refs[:4], refs[4], refs[5:]
    for s in range(4):
        total = came[0][s].astype(f32)
        for ref in came[1:]:
            total += ref[s].astype(f32)
        if s == 0:
            kept[...] = total
        else:
            goes[s - 1][...] = total.astype(bf16)


def reverse_sums(place, near_ref, far_ref, *refs):
    pieces, (out_ref, lhs_ref, held, written) = refs[:-4], refs[-4:]
    n, _, rows = pieces[0].shape
    for r, piece in enumerate(pieces):
        for s in range(n):
            lhs_ref[:, lanes(chip_at(place, -r, -s) * rows, rows)] = piece[s]
    depth = out_ref.shape[0]
    half = depth // 2
    copies = []
    for source, side in ((near_ref, place[0]), (far_ref, 1 - place[0])):
        for pair in range(half // 2):
            at = len(copies)
            total = dot(lhs_ref[...], source[:, pair * 2 * rows : (pair + 1) * 2 * rows])
            for j in range(2):
                held[2 * at + j] = total[:, j * rows : (j + 1) * rows].astype(bf16)
            layer = (2 * (place[1] // 2) + pair * 2 + half * side) % depth
            copies.append(
                pltpu.make_async_copy(
                    held.at[pl.ds(2 * at, 2)], out_ref.at[pl.ds(layer, 2)], written.at[at]
                )
            )
            copies[-1].start()
    for copy in copies:
        copy.wait()


def add_all(column_ref, features_ref, kept_ref, *refs):
    came, out_ref = refs[:-1], refs[-1]
    column = column_ref[0].astype(f32)
    for i in range(1, column_ref.shape[0]):
        column += column_ref[i].astype(f32)
    total = features_ref[...].astype(f32) + kept_ref[...] + column.T
    for ref in came:
        total += ref[...].astype(f32)
    out_ref[...] = total.astype(bf16)


def mlp(values, gain, held, copies, base):
    square = jnp.mean(values * values, axis=-1, keepdims=True)
    normed = (values * lax.rsqrt(square + epsilon) * gain[...]).astype(bf16)
    update = values
    for at in (base, base + 2):
        copies[at].wait()
        u = dot(normed, held[at])
        hidden = (u / (1.0 + jnp.exp(-u))).astype(bf16)
        copies[at + 1].wait()
        update += dot(hidden, held[at + 1])
    return update.astype(bf16)


def update_rows(
    place,
    pre_near,
    pre_far,
    author_near,
    author_far,
    assign_row,
    paper_gain,
    author_gain,
    pw_in,
    pw_in_far,
    pw_out,
    pw_out_far,
    aw_in,
    aw_in_far,
    aw_out,
    aw_out_far,
    paper_out,
    author_out,
    joined,
    held,
    arrived,
):
    sources = (pw_in, pw_out, pw_in_far, pw_out_far, aw_in, aw_out, aw_in_far, aw_out_far)
    copies = [pltpu.make_async_copy(w, held.at[i], arrived.at[i]) for i, w in enumerate(sources)]
    for copy in copies:
        copy.start()
    half = pre_near.shape[1]
    near = lanes(place[0] * half, half)
    far = lanes((1 - place[0]) * half, half)
    joined[:, near] = pre_near[...].astype(f32)
    joined[:, far] = pre_far[...].astype(f32)
    mid = mlp(joined[...], paper_gain, held, copies, 0)
    count_rows = author_near.shape[0]
    papers = mid.shape[0]
    member = assign_row[...] == lax.broadcasted_iota(jnp.int32, (count_rows, papers), 0)
    counts = jnp.sum(member.astype(f32), axis=1, keepdims=True)
    average = dot(member.astype(bf16), mid) / jnp.maximum(counts, 1.0)
    joined[:, near] = author_near[...].astype(f32)
    joined[:, far] = author_far[...].astype(f32)
    author_pre = (joined[...] + average).astype(bf16).astype(f32)
    joined[...] = mid.astype(f32)
    own_mid = joined[:, near]
    final = mlp(author_pre, author_gain, held, copies, 4)
    joined[...] = final.astype(f32)
    own = joined[:, near].astype(bf16)
    author_out[...] = own
    returned = lax.dot_general(
        member.astype(bf16), own, (((0,), (0,)), ((), ())), preferred_element_type=f32
    )
    paper_out[...] = (own_mid + returned).astype(bf16)


def call(kernel, outs, smem, operands, left=(), after=(), scratch=(), limit=16, flops=0, name=None, out_specs=None, moved=None):
    if moved is None:
        moved = sum(2 * a.size for a in (*operands, *left))

    def body(*refs):
        count = len(smem) + len(operands) + len(left)
        return kernel(*refs[:count], *refs[count + len(after) :])

    return pl.pallas_call(
        body,
        out_shape=outs,
        in_specs=[SMEM] * len(smem) + [VMEM] * len(operands) + [HBM] * len(left) + [ANY] * len(after),
        out_specs=out_specs or jax.tree.map(lambda _: VMEM, outs),
        scratch_shapes=list(scratch),
        compiler_params=pltpu.CompilerParams(vmem_limit_bytes=limit * MIB),
        cost_estimate=pl.CostEstimate(flops=flops, bytes_accessed=moved, transcendentals=0),
        name=name or kernel.__name__,
    )(*smem, *operands, *left, *after)


def sent(value, axes, target):
    sizes = [lax.axis_size(a) for a in axes]
    pairs = []
    for at in itertools.product(*(range(n) for n in sizes)):
        to = [i % n for i, n in zip(target(*at), sizes)]
        pairs.append((flat(at, sizes), flat(to, sizes)))
    return lax.ppermute(value, axes, pairs)


def flat(at, sizes):
    index = 0
    for i, n in zip(at, sizes):
        index = index * n + i
    return index


def swap(value):
    return sent(value, ("core",), lambda core: (core + 1,))


def along(value, by, first):
    def target(x, y, core):
        return (x, y + by, core) if (core == 0) == first else (x + by, y, core)

    return sent(value, ("x", "y", "core"), target)


def pair_ahead(pair, ahead):
    return sent(pair, ("z",), lambda z: (z - 2 * ahead,))


def local(
    features,
    partners,
    tiles,
    paper_w_in,
    paper_w_out,
    paper_gain,
    author_feats,
    assign,
    author_w_in,
    author_w_out,
    author_gain,
):
    rows, half = features.shape
    depth = lax.axis_size("z")
    spots = lax.axis_size("x") * lax.axis_size("y")
    wide = depth // 2 * rows
    place = jnp.stack([lax.axis_index(a) for a in ("core", "z", "x", "y")]).astype(jnp.int32)

    turned = features.T
    lines = jnp.stack([turned] + [along(turned, s, True) for s in (1, 2, 3)])
    beside = sent(features, ("z",), lambda z: (z + 1 - 2 * (z % 2),))
    odd = lax.axis_index("z") % 2 == 1
    pair = jnp.stack([jnp.where(odd, beside, features), jnp.where(odd, features, beside)])
    slots = call(
        place_tiles,
        jax.ShapeDtypeStruct((spots, rows, wide), bf16),
        (place, partners[0]),
        (),
        (tiles[0],),
        (),
        [pltpu.VMEM(tiles[0].shape, bf16), pltpu.SemaphoreType.DMA((4,))],
        limit=56,
    )
    slots, pair, lines = lax.optimization_barrier((slots, pair, lines))
    by_plane = [lines] + [along(lines, r, False) for r in (1, 2, 3)]
    column = [pair] + [pair_ahead(pair, i) for i in range(1, depth // 2)]
    near = lax.all_to_all(slots, plane, 0, 0, tiled=True).reshape(spots * rows, wide)
    linked = call(
        join_rows,
        pltpu.HBM((depth * rows, half), bf16),
        (place,),
        tuple(column),
        (),
        (by_plane[1], by_plane[3]),
        [pltpu.VMEM((depth * rows, half), bf16), pltpu.SemaphoreType.DMA],
        out_specs=HBM,
    )
    near, linked = lax.optimization_barrier((near, linked))
    far = swap(near)
    weights = (paper_w_in, paper_w_out, author_w_in, author_w_out)
    weights_far = [swap(w) for w in weights]
    cost = spots * rows * wide * half
    side = len(by_plane)
    line = pltpu.HBM((spots // side, rows, half), bf16)
    token = jax.ShapeDtypeStruct((8, 128), f32)
    *out_plane, ready = call(
        forward_sums,
        [line] * side + [token],
        (place,),
        (near, far, linked),
        (),
        (),
        [pltpu.VMEM((side, *line.shape), bf16), pltpu.SemaphoreType.DMA((side,))],
        limit=20,
        moved=0,
        out_specs=[HBM] * side + [VMEM],
    )
    to_lines = [out_plane[0]] + [along(out_plane[r], r, False) for r in range(1, side)]
    out_column = call(
        reverse_sums,
        pltpu.HBM((depth, half, rows), bf16),
        (place,),
        (near, far, *by_plane),
        (),
        (ready,),
        [
            pltpu.VMEM((half, spots * rows), bf16),
            pltpu.VMEM((depth, half, rows), bf16),
            pltpu.SemaphoreType.DMA((depth // 2,)),
        ],
        limit=20,
        flops=4 * cost,
        out_specs=HBM,
    )
    from_column = lax.all_to_all(out_column, "z", 0, 0, tiled=True)
    kept, *goes = call(
        add_first,
        [jax.ShapeDtypeStruct((rows, half), f32)]
        + [jax.ShapeDtypeStruct((rows, half), bf16)] * (side - 1),
        (),
        tuple(to_lines),
        (),
        tuple(weights_far),
    )
    author_far = swap(author_feats)
    came = [along(v, s, True) for s, v in enumerate(goes, 1)]
    pre = call(
        add_all,
        jax.ShapeDtypeStruct((rows, half), bf16),
        (),
        (from_column, features, kept, *came),
        (),
        (author_far,),
    )
    both = [w for pair_of in zip(weights, weights_far) for w in pair_of]
    return call(
        update_rows,
        (jax.ShapeDtypeStruct((rows, half), bf16), jax.ShapeDtypeStruct((rows, half), bf16)),
        (place,),
        (
            pre,
            swap(pre),
            author_feats,
            author_far,
            assign[None, :],
            paper_gain[None, :],
            author_gain[None, :],
        ),
        tuple(both),
        (),
        [
            pltpu.VMEM((rows, 2 * half), f32),
            pltpu.VMEM((8, 2 * half, 2 * half), bf16),
            pltpu.SemaphoreType.DMA((8,)),
        ],
        limit=58,
        flops=8 * rows * 4 * half * half * 4,
    )


def solution(mesh):
    chips = Mesh(mesh.devices.reshape(8, 4, 4, 2), ("z", "x", "y", "core"))
    blk = ("z", "x", "y")
    placed = (
        P(blk, "core"),
        P(blk, None),
        P(blk, None, None, None),
        P(None, "core"),
        P("core", None),
        P(),
        P(blk, "core"),
        P(blk),
        P(None, "core"),
        P("core", None),
        P(),
    )
    return jax.shard_map(
        local,
        mesh=chips,
        in_specs=placed,
        out_specs=(P(blk, "core"), P(blk, "core")),
        check_vma=False,
    )
```

```python
import functools
import itertools

import jax
import jax.numpy as jnp
from jax import lax
from jax.experimental import pallas as pl
from jax.experimental.pallas import tpu as pltpu
from jax.sharding import Mesh
from jax.sharding import PartitionSpec as P

epsilon = 1e-06
bf16 = jnp.bfloat16
f32 = jnp.float32
plane = ("x", "y")
SMEM = pl.BlockSpec(memory_space=pltpu.SMEM)
VMEM = pl.BlockSpec(memory_space=pltpu.VMEM)
HBM = pl.BlockSpec(memory_space=pltpu.HBM)
ANY = pl.BlockSpec(memory_space=pl.ANY)
MIB = 2**20


def lanes(start, size):
    return pl.ds(pl.multiple_of(start, 128), size)


def dot(left, right):
    return jnp.dot(left, right, preferred_element_type=f32)


def place_tiles(place, ids_ref, tiles_ref, *refs):
    slots_ref, held, arrived = refs[-3:]
    spots, rows, wide = slots_ref.shape
    per_core = wide // rows
    pairs = per_core
    parts = 4
    size = tiles_ref.shape[0] // parts
    copies = [
        pltpu.make_async_copy(
            tiles_ref.at[pl.ds(i * size, size)], held.at[pl.ds(i * size, size)], arrived.at[i]
        )
        for i in range(parts)
    ]
    for copy in copies:
        copy.start()
    slots_ref[...] = jnp.zeros_like(slots_ref)

    first_pair = pairs - (place[1] >> 1)
    first = place[0] * per_core

    def put(f, carry):
        partner = ids_ref[f]
        layer = partner >> spots.bit_length() - 1
        ahead = ((layer >> 1) + first_pair & pairs - 1) * 2 + (layer & 1) - first

        @pl.when((ahead >= 0) & (ahead < per_core))
        def _():
            slots_ref[partner & spots - 1, :, lanes(ahead * rows, rows)] = held[f]

        return carry

    for i, copy in enumerate(copies):
        copy.wait()
        lax.fori_loop(i * size, (i + 1) * size, put, 0, unroll=4)


def write_out(held, out_ref, written):
    copy = pltpu.make_async_copy(held, out_ref, written)
    copy.start()
    copy.wait()


def join_rows(place, *refs):
    blocks, out_ref, held, written = refs[:-3], *refs[-3:]
    rows = blocks[0].shape[1]
    count = len(blocks)
    for i, block in enumerate(blocks):
        spot = (i + place[0] * (count // 2)) % count * 2
        for j in range(2):
            held[pl.ds(pl.multiple_of((spot + j) * rows, rows), rows), :] = block[j]
    write_out(held, out_ref, written)


def chip_at(place, r, s, n=4):
    dx = jnp.where(place[0] == 0, r, s)
    dy = jnp.where(place[0] == 0, s, r)
    return (place[2] + n + dx) % n * n + (place[3] + n + dy) % n


def forward_sums(place, near_ref, far_ref, rhs_ref, *refs):
    outs, ready, held, left = refs[:-3], *refs[-3:]
    ready[...] = jnp.zeros_like(ready)
    width = near_ref.shape[1]
    n, rows, _ = outs[0].shape
    copies = []
    for r, out in enumerate(outs):
        at = [pl.ds(pl.multiple_of(chip_at(place, r, s) * rows, rows), rows) for s in range(n)]
        near = jnp.concatenate([near_ref[a, :] for a in at], axis=0)
        far = jnp.concatenate([far_ref[a, :] for a in at], axis=0)
        total = dot(near, rhs_ref[:width, :]) + dot(far, rhs_ref[width:, :])
        for s in range(n):
            held[r, s] = total[s * rows : (s + 1) * rows, :].astype(bf16)
        copies.append(pltpu.make_async_copy(held.at[r], out, left.at[r]))
        copies[-1].start()
    for copy in copies:
        copy.wait()


def add_first(*refs):
    came, kept, goes = refs[:4], refs[4], refs[5:]
    for s in range(4):
        total = came[0][s].astype(f32)
        for ref in came[1:]:
            total += ref[s].astype(f32)
        if s == 0:
            kept[...] = total
        else:
            goes[s - 1][...] = total.astype(bf16)


def reverse_sums(place, near_ref, far_ref, *refs):
    pieces, (out_ref, lhs_ref, held, written) = refs[:-4], refs[-4:]
    n, _, rows = pieces[0].shape
    for r, piece in enumerate(pieces):
        for s in range(n):
            lhs_ref[:, lanes(chip_at(place, -r, -s) * rows, rows)] = piece[s]
    depth = out_ref.shape[0]
    half = depth // 2
    copies = []
    for source, side in ((near_ref, place[0]), (far_ref, 1 - place[0])):
        for pair in range(half // 2):
            at = len(copies)
            total = dot(lhs_ref[...], source[:, pair * 2 * rows : (pair + 1) * 2 * rows])
            for j in range(2):
                held[2 * at + j] = total[:, j * rows : (j + 1) * rows].astype(bf16)
            layer = (2 * (place[1] // 2) + pair * 2 + half * side) % depth
            copies.append(
                pltpu.make_async_copy(
                    held.at[pl.ds(2 * at, 2)], out_ref.at[pl.ds(layer, 2)], written.at[at]
                )
            )
            copies[-1].start()
    for copy in copies:
        copy.wait()


def add_all(column_ref, features_ref, kept_ref, *refs):
    came, out_ref = refs[:-1], refs[-1]
    column = column_ref[0].astype(f32)
    for i in range(1, column_ref.shape[0]):
        column += column_ref[i].astype(f32)
    total = features_ref[...].astype(f32) + kept_ref[...] + column.T
    for ref in came:
        total += ref[...].astype(f32)
    out_ref[...] = total.astype(bf16)


def mlp(values, gain, held, copies, base):
    square = jnp.mean(values * values, axis=-1, keepdims=True)
    normed = (values * lax.rsqrt(square + epsilon) * gain[...]).astype(bf16)
    update = values
    for at in (base, base + 2):
        copies[at].wait()
        u = dot(normed, held[at])
        hidden = (u / (1.0 + jnp.exp(-u))).astype(bf16)
        copies[at + 1].wait()
        update += dot(hidden, held[at + 1])
    return update.astype(bf16)


def update_rows(
    place,
    pre_near,
    pre_far,
    author_near,
    author_far,
    assign_row,
    paper_gain,
    author_gain,
    pw_in,
    pw_in_far,
    pw_out,
    pw_out_far,
    aw_in,
    aw_in_far,
    aw_out,
    aw_out_far,
    paper_out,
    author_out,
    joined,
    held,
    arrived,
):
    sources = (pw_in, pw_out, pw_in_far, pw_out_far, aw_in, aw_out, aw_in_far, aw_out_far)
    copies = [pltpu.make_async_copy(w, held.at[i], arrived.at[i]) for i, w in enumerate(sources)]
    for copy in copies:
        copy.start()
    half = pre_near.shape[1]
    near = lanes(place[0] * half, half)
    far = lanes((1 - place[0]) * half, half)
    joined[:, near] = pre_near[...].astype(f32)
    joined[:, far] = pre_far[...].astype(f32)
    mid = mlp(joined[...], paper_gain, held, copies, 0)
    count_rows = author_near.shape[0]
    papers = mid.shape[0]
    member = assign_row[...] == lax.broadcasted_iota(jnp.int32, (count_rows, papers), 0)
    counts = jnp.sum(member.astype(f32), axis=1, keepdims=True)
    average = dot(member.astype(bf16), mid) / jnp.maximum(counts, 1.0)
    joined[:, near] = author_near[...].astype(f32)
    joined[:, far] = author_far[...].astype(f32)
    author_pre = (joined[...] + average).astype(bf16).astype(f32)
    joined[...] = mid.astype(f32)
    own_mid = joined[:, near]
    final = mlp(author_pre, author_gain, held, copies, 4)
    joined[...] = final.astype(f32)
    own = joined[:, near].astype(bf16)
    author_out[...] = own
    returned = lax.dot_general(
        member.astype(bf16), own, (((0,), (0,)), ((), ())), preferred_element_type=f32
    )
    paper_out[...] = (own_mid + returned).astype(bf16)


def call(kernel, outs, smem, operands, left=(), after=(), scratch=(), limit=16, flops=0, name=None, out_specs=None, moved=None):
    if moved is None:
        moved = sum(2 * a.size for a in (*operands, *left))

    def body(*refs):
        count = len(smem) + len(operands) + len(left)
        return kernel(*refs[:count], *refs[count + len(after) :])

    return pl.pallas_call(
        body,
        out_shape=outs,
        in_specs=[SMEM] * len(smem) + [VMEM] * len(operands) + [HBM] * len(left) + [ANY] * len(after),
        out_specs=out_specs or jax.tree.map(lambda _: VMEM, outs),
        scratch_shapes=list(scratch),
        compiler_params=pltpu.CompilerParams(vmem_limit_bytes=limit * MIB),
        cost_estimate=pl.CostEstimate(flops=flops, bytes_accessed=moved, transcendentals=0),
        name=name or kernel.__name__,
    )(*smem, *operands, *left, *after)


def sent(value, axes, target):
    sizes = [lax.axis_size(a) for a in axes]
    pairs = []
    for at in itertools.product(*(range(n) for n in sizes)):
        to = [i % n for i, n in zip(target(*at), sizes)]
        pairs.append((flat(at, sizes), flat(to, sizes)))
    return lax.ppermute(value, axes, pairs)


def flat(at, sizes):
    index = 0
    for i, n in zip(at, sizes):
        index = index * n + i
    return index


def swap(value):
    return sent(value, ("core",), lambda core: (core + 1,))


def along(value, by, first):
    def target(x, y, core):
        return (x, y + by, core) if (core == 0) == first else (x + by, y, core)

    return sent(value, ("x", "y", "core"), target)


def pair_ahead(pair, ahead):
    return sent(pair, ("z",), lambda z: (z - 2 * ahead,))


def local(
    features,
    partners,
    tiles,
    paper_w_in,
    paper_w_out,
    paper_gain,
    author_feats,
    assign,
    author_w_in,
    author_w_out,
    author_gain,
):
    rows, half = features.shape
    depth = lax.axis_size("z")
    spots = lax.axis_size("x") * lax.axis_size("y")
    wide = depth // 2 * rows
    place = jnp.stack([lax.axis_index(a) for a in ("core", "z", "x", "y")]).astype(jnp.int32)

    turned = features.T
    lines = jnp.stack([turned] + [along(turned, s, True) for s in (1, 2, 3)])
    beside = sent(features, ("z",), lambda z: (z + 1 - 2 * (z % 2),))
    odd = lax.axis_index("z") % 2 == 1
    pair = jnp.stack([jnp.where(odd, beside, features), jnp.where(odd, features, beside)])
    slots = call(
        place_tiles,
        jax.ShapeDtypeStruct((spots, rows, wide), bf16),
        (place, partners[0]),
        (),
        (tiles[0],),
        (),
        [pltpu.VMEM(tiles[0].shape, bf16), pltpu.SemaphoreType.DMA((4,))],
        limit=56,
    )
    slots, pair, lines = lax.optimization_barrier((slots, pair, lines))
    by_plane = [lines] + [along(lines, r, False) for r in (1, 2, 3)]
    column = [pair] + [pair_ahead(pair, i) for i in range(1, depth // 2)]
    near = lax.all_to_all(slots, plane, 0, 0, tiled=True).reshape(spots * rows, wide)
    linked = call(
        join_rows,
        pltpu.HBM((depth * rows, half), bf16),
        (place,),
        tuple(column),
        (),
        (by_plane[1], by_plane[3]),
        [pltpu.VMEM((depth * rows, half), bf16), pltpu.SemaphoreType.DMA],
        out_specs=HBM,
    )
    near, linked = lax.optimization_barrier((near, linked))
    far = swap(near)
    weights = (paper_w_in, paper_w_out, author_w_in, author_w_out)
    weights_far = [swap(w) for w in weights]
    cost = spots * rows * wide * half
    side = len(by_plane)
    line = pltpu.HBM((spots // side, rows, half), bf16)
    token = jax.ShapeDtypeStruct((8, 128), f32)
    *out_plane, ready = call(
        forward_sums,
        [line] * side + [token],
        (place,),
        (near, far, linked),
        (),
        (),
        [pltpu.VMEM((side, *line.shape), bf16), pltpu.SemaphoreType.DMA((side,))],
        limit=20,
        moved=0,
        out_specs=[HBM] * side + [VMEM],
    )
    to_lines = [out_plane[0]] + [along(out_plane[r], r, False) for r in range(1, side)]
    out_column = call(
        reverse_sums,
        pltpu.HBM((depth, half, rows), bf16),
        (place,),
        (near, far, *by_plane),
        (),
        (ready,),
        [
            pltpu.VMEM((half, spots * rows), bf16),
            pltpu.VMEM((depth, half, rows), bf16),
            pltpu.SemaphoreType.DMA((depth // 2,)),
        ],
        limit=20,
        flops=4 * cost,
        out_specs=HBM,
    )
    from_column = lax.all_to_all(out_column, "z", 0, 0, tiled=True)
    kept, *goes = call(
        add_first,
        [jax.ShapeDtypeStruct((rows, half), f32)]
        + [jax.ShapeDtypeStruct((rows, half), bf16)] * (side - 1),
        (),
        tuple(to_lines),
        (),
        tuple(weights_far),
    )
    author_far = swap(author_feats)
    came = [along(v, s, True) for s, v in enumerate(goes, 1)]
    pre = call(
        add_all,
        jax.ShapeDtypeStruct((rows, half), bf16),
        (),
        (from_column, features, kept, *came),
        (),
        (author_far,),
    )
    both = [w for pair_of in zip(weights, weights_far) for w in pair_of]
    return call(
        update_rows,
        (jax.ShapeDtypeStruct((rows, half), bf16), jax.ShapeDtypeStruct((rows, half), bf16)),
        (place,),
        (
            pre,
            swap(pre),
            author_feats,
            author_far,
            assign[None, :],
            paper_gain[None, :],
            author_gain[None, :],
        ),
        tuple(both),
        (),
        [
            pltpu.VMEM((rows, 2 * half), f32),
            pltpu.VMEM((8, 2 * half, 2 * half), bf16),
            pltpu.SemaphoreType.DMA((8,)),
        ],
        limit=53,
        flops=8 * rows * 4 * half * half * 4,
    )


def solution(mesh):
    chips = Mesh(mesh.devices.reshape(8, 4, 4, 2), ("z", "x", "y", "core"))
    blk = ("z", "x", "y")
    placed = (
        P(blk, "core"),
        P(blk, None),
        P(blk, None, None, None),
        P(None, "core"),
        P("core", None),
        P(),
        P(blk, "core"),
        P(blk),
        P(None, "core"),
        P("core", None),
        P(),
    )
    return jax.shard_map(
        local,
        mesh=chips,
        in_specs=placed,
        out_specs=(P(blk, "core"), P(blk, "core")),
        check_vma=False,
    )
```
